128 devices in a mesh: seq: 32 (over z, y, core), head: 4 (over x).
Axes of the slice: x: 4, y: 4, z: 4, core: 2. Of those that a mesh axis runs over, the one named last changes fastest.
Arguments:
- hidden_in: bfloat16 [8192, 2048], P('seq', 'head'), may hold values from -6 to 6
- out_grad: bfloat16 [8192, 2048], P('seq', 'head'), may hold values from -6 to 6
- norm_attn: float32 [2048], replicated, may hold values from 0.5 to 1.5
- w_query: bfloat16 [2048, 2048], P('seq', 'head'), may hold values from -0.125 to 0.125
- w_key: bfloat16 [2048, 2048], P('seq', 'head'), may hold values from -0.125 to 0.125
- w_value: bfloat16 [2048, 4096], P('seq', 'head'), may hold values from -0.125 to 0.125
- conv_query: bfloat16 [4, 2048], P(None, 'head'), may hold values from -3 to 3
- conv_key: bfloat16 [4, 2048], P(None, 'head'), may hold values from -3 to 3
- conv_value: bfloat16 [4, 4096], P(None, 'head'), may hold values from -3 to 3
- w_alpha: bfloat16 [2048, 16], P('seq', 'head'), may hold values from -0.125 to 0.125
- w_beta: bfloat16 [2048, 16], P('seq', 'head'), may hold values from -0.125 to 0.125
- log_rate: float32 [16], P('head'), may hold values from -12 to -2
- rate_bias: float32 [16], P('head'), may hold values from -1 to 1
- w_gate_out: bfloat16 [2048, 4096], P('seq', 'head'), may hold values from -0.125 to 0.125
- head_norm: float32 [256], replicated, may hold values from 0.5 to 1.5
- w_out: bfloat16 [4096, 2048], P('head', 'seq'), may hold values from -0.1875 to 0.1875
- norm_mlp: float32 [2048], replicated, may hold values from 0.5 to 1.5
- w_mlp_gate: bfloat16 [2048, 5504], P('seq', 'head'), may hold values from -0.125 to 0.125
- w_mlp_up: bfloat16 [2048, 5504], P('seq', 'head'), may hold values from -0.125 to 0.125
- w_mlp_down: bfloat16 [5504, 2048], P('head', 'seq'), may hold values from -0.15625 to 0.15625
Outputs:
- output: bfloat16 [8192, 2048], P('seq', 'head')
- grad_input: bfloat16 [8192, 2048], P('seq', 'head')
- grad_norm_attn: float32 [2048], replicated
- grad_query: float32 [2048, 2048], P('seq', 'head')
- grad_key: float32 [2048, 2048], P('seq', 'head')
- grad_value: float32 [2048, 4096], P('seq', 'head')
- grad_conv_query: float32 [4, 2048], P(None, 'head')
- grad_conv_key: float32 [4, 2048], P(None, 'head')
- grad_conv_value: float32 [4, 4096], P(None, 'head')
- grad_alpha: float32 [2048, 16], P('seq', 'head')
- grad_beta: float32 [2048, 16], P('seq', 'head')
- grad_log_rate: float32 [16], P('head')
- grad_rate_bias: float32 [16], P('head')
- grad_gate_out: float32 [2048, 4096], P('seq', 'head')
- grad_head_norm: float32 [256], replicated
- grad_out: float32 [4096, 2048], P('head', 'seq')
- grad_norm_mlp: float32 [2048], replicated
- grad_mlp_gate: float32 [2048, 5504], P('seq', 'head')
- grad_mlp_up: float32 [2048, 5504], P('seq', 'head')
- grad_mlp_down: float32 [5504, 2048], P('head', 'seq')
The draws below stay inside these ranges and needn't reach their ends.
All inputs are finite; a program needn't handle non-finite values.
Results may differ from the reference program's by a relative error of at most 0.038.
Values may be sent and summed in bfloat16 or wider, within the bound.
No kernel may reach another device: no remote copies, remote signals or barrier semaphores. Data moves between devices by JAX's collectives and lax.ppermute only.
A program may use at most 256 MiB of HBM per device.

```python
import jax
import jax.numpy as jnp
from jax import lax

D = 2048
HEADS = 16
DK = 128
DV = 256
FF = 5504
CONV = 4
BLOCK = 64
TOKENS = 8192


def draw_log_rate(key, part):
    key = jax.random.fold_in(key, 11)
    pick_key, slow_key, fast_key = jax.random.split(key, 3)
    share = 0.55
    slow_rates = jax.random.uniform(slow_key, (HEADS,), jnp.float32, jnp.log(0.3 / TOKENS), jnp.log(3.0 / TOKENS))
    fast_rates = jax.random.uniform(fast_key, (HEADS,), jnp.float32, jnp.log(0.02), jnp.log(0.06))
    chosen = jax.random.uniform(pick_key, (HEADS,), jnp.float32) < share
    return jnp.where(chosen, slow_rates, fast_rates)


def block_levels(stream_key, extent, cuts, low, top_value):
    gain = 1.0
    for axis_at, shards_of in cuts:
        draws = jax.random.uniform(jax.random.fold_in(jax.random.fold_in(stream_key, 6), axis_at), (shards_of,), jnp.float32, low / len(cuts), top_value / len(cuts))
        gain = gain * jnp.repeat(jnp.exp(draws), extent[axis_at] // shards_of).reshape((-1,) + (1,) * (len(extent) - 1 - axis_at))
    return gain


def scatter_about(rng, extent, deviation, most, shards=(), held_as=jnp.bfloat16):
    values = jax.random.normal(rng, extent, jnp.float32) * deviation
    if len(shards) > 0:
        values = block_levels(rng, extent, shards, -0.22, 0.18) * values
    return jnp.clip(values, min=-most, max=most).astype(held_as)


def setup_inputs(seed: int = 0) -> dict:
    streams_of = jax.random.split(jax.random.key(seed), 21)
    return {
        "hidden_in": scatter_about(streams_of[0], (TOKENS, D), 1.0, 6.0, ((0, 32), (1, 4))),
        "out_grad": scatter_about(streams_of[1], (TOKENS, D), 1.0, 6.0, ((0, 32), (1, 4))),
        "norm_attn": jnp.clip(1.0 + 0.1 * jax.random.normal(streams_of[2], (D,), jnp.float32), 0.5, 1.5),
        "w_query": scatter_about(streams_of[3], (D, HEADS * DK), D ** -0.5, 0.125, ((0, 32), (1, 4))),
        "w_key": scatter_about(streams_of[4], (D, HEADS * DK), D ** -0.5, 0.125, ((0, 32), (1, 4))),
        "w_value": scatter_about(streams_of[5], (D, HEADS * DV), D ** -0.5, 0.125, ((0, 32), (1, 4))),
        "conv_query": scatter_about(streams_of[6], (CONV, HEADS * DK), CONV ** -0.5, 3.0, ((1, 4),)),
        "conv_key": scatter_about(streams_of[7], (CONV, HEADS * DK), CONV ** -0.5, 3.0, ((1, 4),)),
        "conv_value": scatter_about(streams_of[8], (CONV, HEADS * DV), CONV ** -0.5, 3.0, ((1, 4),)),
        "w_alpha": scatter_about(streams_of[9], (D, HEADS), D ** -0.5, 0.125, ((0, 32), (1, 4))),
        "w_beta": scatter_about(streams_of[10], (D, HEADS), D ** -0.5, 0.125, ((0, 32), (1, 4))),
        "log_rate": draw_log_rate(jax.random.fold_in(streams_of[20], 71), 0),
        "rate_bias": jnp.clip(jax.random.uniform(streams_of[12], (HEADS,), jnp.float32, -1.0, 1.0) * block_levels(streams_of[12], (HEADS,), ((0, 4),), -0.4, 0.0), -1.0, 1.0),
        "w_gate_out": scatter_about(streams_of[13], (D, HEADS * DV), D ** -0.5, 0.125, ((0, 32), (1, 4))),
        "head_norm": jnp.clip(1.0 + 0.1 * jax.random.normal(streams_of[14], (DV,), jnp.float32), 0.5, 1.5),
        "w_out": scatter_about(streams_of[15], (HEADS * DV, D), (HEADS * DV // 4) ** -0.5, 0.1875, ((0, 4), (1, 32))),
        "norm_mlp": jnp.clip(1.0 + 0.1 * jax.random.normal(streams_of[16], (D,), jnp.float32), 0.5, 1.5),
        "w_mlp_gate": scatter_about(streams_of[17], (D, FF), D ** -0.5, 0.125, ((0, 32), (1, 4))),
        "w_mlp_up": scatter_about(streams_of[18], (D, FF), D ** -0.5, 0.125, ((0, 32), (1, 4))),
        "w_mlp_down": scatter_about(streams_of[19], (FF, D), (FF // 4) ** -0.5, 0.15625, ((0, 4), (1, 32))),
    }


EPSILON = 1e-06
EXACT_PRECISION = lax.Precision.HIGHEST

@jax.custom_vjp
def low(v):
    return lax.optimization_barrier(v.astype(jnp.bfloat16)).astype(jnp.float32)

@jax.custom_vjp
def low_back(v):
    return v

def low_keep(v):
    return (low(v), None)

def low_pass(kept, grad):
    return (grad,)

def back_keep(v):
    return (v, None)

def back_low(kept, grad):
    return (low(grad),)
low.defvjp(low_keep, low_pass)
low_back.defvjp(back_keep, back_low)

def matmul(left_op, right_op):
    return jnp.dot(left_op.astype(jnp.float32), right_op.astype(jnp.float32), precision=EXACT_PRECISION, preferred_element_type=jnp.float32)

def rms_gain(rows_in, gain_vec):
    factor = lax.rsqrt(lax.optimization_barrier(jnp.mean(rows_in * rows_in, axis=-1, keepdims=True)) + EPSILON)
    return rows_in * factor * gain_vec

def unit_rows(rows_in):
    return rows_in * lax.rsqrt(lax.optimization_barrier(jnp.sum(rows_in * rows_in, axis=-1, keepdims=True)) + EPSILON)

def conv_silu(projected, taps_w):
    tap_count = taps_w.shape[0]
    row_count = projected.shape[0]
    padded = jnp.concatenate([jnp.zeros((tap_count - 1, projected.shape[1]), jnp.float32), projected], 0)
    conv_out = padded[0:row_count] * taps_w[0]
    for position in range(1, tap_count):
        conv_out = conv_out + padded[position:position + row_count] * taps_w[position]
    return jax.nn.silu(conv_out)

def delta_rule(queries, key_rows, values, log_decay, beta_rows):
    row_count, head_count, key_dimension = key_rows.shape
    value_size = values.shape[2]
    blocks = row_count // BLOCK

    def to_blocks(array_in):
        return jnp.swapaxes(array_in.reshape((blocks, BLOCK) + array_in.shape[1:]), 1, 2)
    causal_mask = jnp.tril(jnp.ones((BLOCK, BLOCK), dtype=bool))
    strict_mask = jnp.tril(jnp.ones((BLOCK, BLOCK), dtype=bool), -1)
    identity = jnp.eye(BLOCK, dtype=jnp.float32)

    def advance(running_state, block_in):
        query_portion, key_part, value_part, rate_part, beta_part = block_in
        cumulative = jnp.cumsum(rate_part, axis=-1)
        log_gap = cumulative[:, :, None] - cumulative[:, None, :]
        decay_ratio = jnp.exp(jnp.where(causal_mask, log_gap, 0.0))
        key_gram = jnp.einsum('hck,hdk->hcd', key_part, key_part, precision=EXACT_PRECISION)
        system = identity + beta_part[:, :, None] * jnp.where(strict_mask, key_gram * decay_ratio, 0.0)
        decay_factor_rows = jnp.exp(cumulative)
        right_side = beta_part[:, :, None] * jnp.concatenate([key_part * decay_factor_rows[:, :, None], value_part], -1)
        solved = lax.linalg.triangular_solve(system, right_side, left_side=True, lower=True, unit_diagonal=True)
        weight_matrix_rows = solved[..., :key_dimension]
        surrogate_rows = solved[..., key_dimension:]
        update_term_rows = surrogate_rows - jnp.einsum('oum,omn->oun', weight_matrix_rows, running_state, precision=EXACT_PRECISION)
        query_key = jnp.where(causal_mask, jnp.einsum('hck,hdk->hcd', query_portion, key_part, precision=EXACT_PRECISION) * decay_ratio, 0.0)
        output_rows = jnp.einsum('oum,omn->oun', query_portion * decay_factor_rows[:, :, None], running_state, precision=EXACT_PRECISION)
        output_rows = output_rows + jnp.einsum('hcd,hdv->hcv', query_key, update_term_rows, precision=EXACT_PRECISION)
        trailing_keys = key_part * jnp.exp(cumulative[:, -1:] - cumulative)[:, :, None]
        updated_state = jnp.exp(cumulative[:, -1])[:, None, None] * running_state
        updated_state = updated_state + jnp.einsum('moe,mol->mel', trailing_keys, update_term_rows, precision=EXACT_PRECISION)
        return (updated_state, output_rows)
    inputs_all = (to_blocks(queries), to_blocks(key_rows), to_blocks(values), to_blocks(log_decay), to_blocks(beta_rows))
    start_state = jnp.zeros((head_count, key_dimension, value_size), jnp.float32)
    final_state, block_outs = lax.scan(jax.checkpoint(advance), start_state, inputs_all)
    return jnp.swapaxes(block_outs, 1, 2).reshape(row_count, head_count, value_size)

def layer_forward(hidden_in, norm_attn, w_query, w_key, w_value, conv_query, conv_key, conv_value, w_alpha, w_beta, log_rate, rate_bias, w_gate_out, head_norm, w_out, norm_mlp, w_mlp_gate, w_mlp_up, w_mlp_down):
    row_count = hidden_in.shape[0]
    normed = low(rms_gain(hidden_in, norm_attn))
    q_raw = low_back(low(matmul(normed, w_query)))
    k_raw = low_back(low(matmul(normed, w_key)))
    v_raw = low_back(low(matmul(normed, w_value)))
    alpha_in = low_back(matmul(normed, w_alpha))
    beta_in = low_back(matmul(normed, w_beta))
    gate_in = low_back(matmul(normed, w_gate_out))
    queries = low_back(low(unit_rows(conv_silu(q_raw, conv_query).reshape(row_count, HEADS, DK)) * DK ** (-0.5)))
    key_rows = low_back(low(unit_rows(conv_silu(k_raw, conv_key).reshape(row_count, HEADS, DK))))
    values = low_back(low(conv_silu(v_raw, conv_value).reshape(row_count, HEADS, DV)))
    log_decay = -jnp.exp(log_rate) * jax.nn.softplus(alpha_in + rate_bias)
    beta_rows = jax.nn.sigmoid(beta_in)
    mixture_output = delta_rule(queries, key_rows, values, log_decay, beta_rows)
    gated = mixture_output * lax.rsqrt(lax.optimization_barrier(jnp.mean(mixture_output * mixture_output, axis=-1, keepdims=True)) + EPSILON) * head_norm
    gated = gated * jax.nn.silu(gate_in.reshape(row_count, HEADS, DV))
    attn = low(gated.reshape(row_count, HEADS * DV))
    middle = low_back(low(hidden_in + matmul(attn, w_out)))
    normed_two = low(rms_gain(middle, norm_mlp))
    gate_rows = low_back(matmul(normed_two, w_mlp_gate))
    up_rows = low_back(matmul(normed_two, w_mlp_up))
    inner = low(jax.nn.silu(gate_rows) * up_rows)
    return middle + matmul(inner, w_mlp_down)

def reference(hidden_in, out_grad, norm_attn, w_query, w_key, w_value, conv_query, conv_key, conv_value, w_alpha, w_beta, log_rate, rate_bias, w_gate_out, head_norm, w_out, norm_mlp, w_mlp_gate, w_mlp_up, w_mlp_down):
    as_float = jnp.float32
    output, pullback = jax.vjp(layer_forward, hidden_in.astype(as_float), norm_attn.astype(as_float), w_query.astype(as_float), w_key.astype(as_float), w_value.astype(as_float), conv_query.astype(as_float), conv_key.astype(as_float), conv_value.astype(as_float), w_alpha.astype(as_float), w_beta.astype(as_float), log_rate.astype(as_float), rate_bias.astype(as_float), w_gate_out.astype(as_float), head_norm.astype(as_float), w_out.astype(as_float), norm_mlp.astype(as_float), w_mlp_gate.astype(as_float), w_mlp_up.astype(as_float), w_mlp_down.astype(as_float))
    grad_input, grad_norm_attn, grad_query, grad_key, grad_value, grad_conv_query, grad_conv_key, grad_conv_value, grad_alpha, grad_beta, grad_log_rate, grad_rate_bias, grad_gate_out, grad_head_norm, grad_out, grad_norm_mlp, grad_mlp_gate, grad_mlp_up, grad_mlp_down = pullback(out_grad.astype(as_float))
    return (output.astype(jnp.bfloat16), grad_input.astype(jnp.bfloat16), grad_norm_attn, grad_query, grad_key, grad_value, grad_conv_query, grad_conv_key, grad_conv_value, grad_alpha, grad_beta, grad_log_rate, grad_rate_bias, grad_gate_out, grad_head_norm, grad_out, grad_norm_mlp, grad_mlp_gate, grad_mlp_up, grad_mlp_down)
```

```python
from functools import partial

import jax
import jax.numpy as jnp
from jax import lax
from jax.experimental import pallas as pl
from jax.experimental.pallas import tpu as pltpu
from jax.sharding import PartitionSpec as P

EPSILON = 1e-06
F32 = jnp.float32
BF16 = jnp.bfloat16
C = 128
DK = 128
DV = 256
H = 2
TAPS = 4
VMEM = 56 * 1024 * 1024
NZ, NY, NC = 4, 4, 2
NX = 4
PAIR = 2
ROWS = PAIR * C


def mm(a, b):
    return jnp.dot(a.astype(BF16), b.astype(BF16), preferred_element_type=F32)


def nt(a, b):
    return lax.dot_general(
        a.astype(BF16), b.astype(BF16), (((1,), (1,)), ((), ())), preferred_element_type=F32
    )


def tn(a, b):
    return lax.dot_general(
        a.astype(BF16), b.astype(BF16), (((0,), (0,)), ((), ())), preferred_element_type=F32
    )


def halves(b):
    hi = b.astype(BF16)
    return hi, (b - hi.astype(F32)).astype(BF16)


def mm_two(a, b):
    hi, lo = halves(b)
    return mm(a, hi) + mm(a, lo)


def tn_two(a, b):
    hi, lo = halves(b)
    return tn(a, hi) + tn(a, lo)


def mm_three(a, b):
    a_hi, a_lo = halves(a)
    b_hi, b_lo = halves(b)
    return mm(a_hi, b_hi) + (mm(a_hi, b_lo) + mm(a_lo, b_hi))


def mm_ones(ones, b):
    hi, rest = halves(b)
    low = (b - hi.astype(F32)) - rest.astype(F32)
    return mm(ones, hi) + (mm(ones, rest) + mm(ones, low))


def iotas(rows, columns):
    return (
        lax.broadcasted_iota(jnp.int32, (rows, columns), 0),
        lax.broadcasted_iota(jnp.int32, (rows, columns), 1),
    )


def unit_lower_inverse(lows):
    row, col = iotas(C, C)
    eye = (row == col).astype(F32)
    same = (row >> 3) == (col >> 3)
    base = [jnp.where(same, n, 0.0) for n in lows]
    square = [mm(b, b) for b in base]
    cross = [mm(b, s) for b, s in zip(base, square)]
    fourth = [mm(s, s) for s in square]
    partial_inv = [eye - b + s - c for b, s, c in zip(base, square, cross)]
    extra = [mm(p, f) for p, f in zip(partial_inv, fourth)]
    inverse = [p + e for p, e in zip(partial_inv, extra)]
    level = 3
    while (1 << level) < C:
        pair = ((row >> (level + 1)) == (col >> (level + 1))) & ((row >> level) != (col >> level))
        off = [jnp.where(pair, n, 0.0) for n in lows]
        right = [mm(o, t) for o, t in zip(off, inverse)]
        step = [mm(t, r) for t, r in zip(inverse, right)]
        inverse = [t - s for t, s in zip(inverse, step)]
        level += 1
    residual = [eye - t - mm_three(n, t) for n, t in zip(lows, inverse)]
    fix = [mm(t, r) for t, r in zip(inverse, residual)]
    return [t + f for t, f in zip(inverse, fix)]


def conv_apply(window, taps):
    count = window.shape[0] - 16
    out = window[13 : 13 + count] * taps[0:1]
    for j in range(1, TAPS):
        out = out + window[13 + j : 13 + j + count] * taps[j : j + 1]
    return out


def conv_window(before, current):
    return jnp.concatenate([before, current], 0).astype(BF16).astype(F32)


def softplus(v):
    return jnp.maximum(v, 0.0) + jnp.log1p(jnp.exp(-jnp.abs(v)))


def gates_of(ab, rates):
    row, col = iotas(C, C)
    log_decay = rates[0:1] * softplus(ab + rates[1:2])
    cumulative = mm_ones((row >= col).astype(F32), log_decay)
    return jnp.where(col < H, cumulative, jax.nn.sigmoid(ab))


def decay_ratio(column, line):
    row, col = iotas(C, C)
    return jnp.exp(jnp.where(row >= col, column - line, 0.0))


def block(j):
    return slice(j * C, (j + 1) * C)


def head_keys(h):
    return slice(h * DK, (h + 1) * DK)


def head_values(h):
    return slice(h * DV, (h + 1) * DV)


CHAINS = [(j, h) for j in range(PAIR) for h in range(H)]


def chunk_forward_kernel(
    where_ref, x_ref, before_ref, edge_ref, ab_ref, taps_ref, rates_ref,
    q_ref, k_ref, v_ref, gates_ref, p_ref, t_ref, w_ref, u_ref, map_ref, state,
):
    n = pl.program_id(0)
    row, col = iotas(C, C)
    before = jnp.where(n == 0, edge_ref[...], before_ref[...])
    window = conv_window(before, x_ref[...])
    conv = conv_apply(window, taps_ref[...])
    act = conv * jax.nn.sigmoid(conv)
    all_gates = [gates_of(ab_ref[block(j)], rates_ref[...]) for j in range(PAIR)]
    lines = [a.T for a in all_gates]
    for j in range(PAIR):
        gates_ref[block(j)] = all_gates[j]
    qs, ks, vs = [], [], []
    for h in range(H):
        q = act[:, head_keys(h)]
        k = act[:, head_keys(H + h)]
        q = q * lax.rsqrt(jnp.sum(q * q, -1, keepdims=True) + EPSILON) * DK ** (-0.5)
        k = k * lax.rsqrt(jnp.sum(k * k, -1, keepdims=True) + EPSILON)
        qs.append(q.astype(BF16))
        ks.append(k.astype(BF16))
        vs.append(act[:, 2 * H * DK + h * DV : 2 * H * DK + (h + 1) * DV].astype(BF16))
        q_ref[:, head_keys(h)] = qs[h]
        k_ref[:, head_keys(h)] = ks[h]
        v_ref[:, head_values(h)] = vs[h]
    q = [qs[h][block(j)] for j, h in CHAINS]
    k = [ks[h][block(j)] for j, h in CHAINS]
    v = [vs[h][block(j)] for j, h in CHAINS]
    g = [all_gates[j][:, h : h + 1] for j, h in CHAINS]
    beta = [all_gates[j][:, H + h : H + h + 1] for j, h in CHAINS]
    ratio = [decay_ratio(g[c], lines[j][h : h + 1]) for c, (j, h) in enumerate(CHAINS)]
    chains = range(len(CHAINS))
    gram = [nt(k[c], k[c]) for c in chains]
    score = [nt(q[c], k[c]) for c in chains]
    low = [beta[c] * jnp.where(row > col, gram[c] * ratio[c], 0.0) for c in chains]
    inverse = [t.astype(BF16) for t in unit_lower_inverse(low)]
    growth = [jnp.exp(g[c]) for c in chains]
    wide_k = [k[c].astype(F32) * (beta[c] * growth[c]) for c in chains]
    wide_v = [v[c].astype(F32) * beta[c] for c in chains]
    w = [mm(inverse[c], wide_k[c]).astype(BF16) for c in chains]
    u = [mm(inverse[c], wide_v[c]) for c in chains]
    for c, (j, h) in enumerate(CHAINS):
        p_ref[j, h] = jnp.where(row >= col, score[c] * ratio[c], 0.0).astype(BF16)
        t_ref[j, h] = inverse[c]
        w_ref[j, h] = w[c]
        u_ref[j, h] = u[c]

    @pl.when(n == 0)
    def _():
        for h in range(H):
            state[h] = jnp.concatenate(
                [(row == col).astype(F32), jnp.zeros((DK, DV), F32)], 1
            )

    for c, (j, h) in enumerate(CHAINS):
        old = state[h]
        total = g[c][C - 1 : C]
        trail = k[c].astype(F32) * jnp.exp(total - g[c])
        delta = jnp.concatenate([jnp.zeros((C, DK), F32), u[c]], 1) - mm(w[c], old)
        state[h] = jnp.exp(total) * old + tn(trail, delta)

    @pl.when(n == pl.num_programs(0) - 1)
    def _():
        map_ref[...] = state[...].astype(BF16)


def ring_parts(refs):
    own, one, top, bottom, three = refs
    return [
        [own.at[0], own.at[1]], [one.at[0], one.at[1]],
        [top.at[0], bottom.at[0]], [three.at[0], three.at[1]],
    ]


def line_map_kernel(place_ref, *refs):
    y = place_ref[0]
    parts, (out_ref, held) = ring_parts(refs[:5]), refs[5:]
    for k in range(NY):
        for h in range(H):
            held[k, h] = parts[k][h][...]
    totals = [held[y, h].astype(F32) for h in range(H)]
    for j in range(1, NY):
        k = lax.rem(y - j + NY, NY)
        for h in range(H):
            new = held[k, h]
            totals[h] = mm_two(new[:, :DK], totals[h]) + jnp.concatenate(
                [jnp.zeros((DK, DK), F32), new[:, DK:].astype(F32)], 1
            )
    for h in range(H):
        out_ref[h] = totals[h].astype(BF16)


def chunk_output_kernel(where_ref, *refs):
    along, across, refs = ring_parts(refs[:5]), ring_parts(refs[5:10]), refs[10:]
    (q_ref, k_ref, gates_ref, p_ref, w_ref, u_ref, gate_ref, gain_ref,
     mixed_ref, attn_ref, d_ref, s_ref, state) = refs
    n = pl.program_id(0)
    y, z = where_ref[1], where_ref[2]

    @pl.when(n == 0)
    def _():
        s = [jnp.zeros((DK, DV), F32) for _ in range(H)]
        for place, maps in ((z, across), (y, along)):
            for shift in (3, 2, 1):
                for h in range(H):
                    m = maps[shift][h]
                    new = mm_two(m[:, :DK], s[h]) + m[:, DK:].astype(F32)
                    s[h] = jnp.where(place >= shift, new, s[h])
        for h in range(H):
            state[h] = s[h]

    gain = gain_ref[...]
    for j, h in CHAINS:
        g = gates_ref[block(j), h : h + 1]
        total = g[C - 1 : C]
        s = state[h]
        held = s.astype(BF16)
        s_ref[j, h] = held
        q = q_ref[block(j), head_keys(h)].astype(F32) * jnp.exp(g)
        delta = (u_ref[j, h] - mm(w_ref[j, h], held)).astype(BF16)
        d_ref[j, h] = delta
        out = mm(q, held) + mm(p_ref[j, h], delta)
        trail = k_ref[block(j), head_keys(h)].astype(F32) * jnp.exp(total - g)
        state[h] = jnp.exp(total) * s + tn(trail, delta)
        mixed_ref[block(j), head_values(h)] = out
        gate = gate_ref[block(j), head_values(h)]
        r = lax.rsqrt(jnp.mean(out * out, -1, keepdims=True) + EPSILON)
        attn = out * r * gain * (gate * jax.nn.sigmoid(gate))
        attn_ref[block(j), head_values(h)] = attn.astype(BF16)


def chunk_adjoint_kernel(
    where_ref, own_ref, other_ref, wa_ref, mixed_ref, gate_ref, gain_ref, q_ref, k_ref,
    gates_ref, p_ref, w_ref,
    dm_ref, dg_ref, gain_out_ref, pd_ref, qd_ref, n_ref, state,
):
    i = pl.program_id(0)
    last = pl.num_programs(0) - 1

    @pl.when(i == 0)
    def _():
        state[...] = jnp.zeros_like(state)
        gain_out_ref[...] = jnp.zeros_like(gain_out_ref)

    mine = (last - i) == where_ref[0]
    d_attn = mm(jnp.where(mine, own_ref[...], other_ref[...]), wa_ref[...])
    gain = gain_ref[...]
    for j, h in reversed(CHAINS):
        rows, cols = block(j), head_values(h)
        da, mixed, gate = d_attn[rows, cols], mixed_ref[rows, cols], gate_ref[rows, cols]
        r = lax.rsqrt(jnp.mean(mixed * mixed, -1, keepdims=True) + EPSILON)
        m = mixed * r
        s = jax.nn.sigmoid(gate)
        z = gate * s
        e = da * gain * z
        dm = (r * (e - m * jnp.mean(e * m, -1, keepdims=True))).astype(BF16)
        dm_ref[rows, cols] = dm
        dg_ref[rows, cols] = (da * gain * m * (s * (1.0 + gate * (1.0 - s)))).astype(BF16)
        gain_out_ref[0:1] += jnp.sum(da * m * z, 0, keepdims=True)
        g = gates_ref[rows, h : h + 1]
        total = g[C - 1 : C]
        q = q_ref[rows, head_keys(h)].astype(F32) * jnp.exp(g)
        trail = k_ref[rows, head_keys(h)].astype(F32) * jnp.exp(total - g)
        p_dm, q_dm = tn(p_ref[j, h], dm), tn(q, dm)
        pd_ref[j, h], qd_ref[j, h] = p_dm, q_dm
        old = state[h]
        state[h] = jnp.exp(total) * old + q_dm - tn(w_ref[j, h], p_dm + mm(trail, old))

    @pl.when(i == last)
    def _():
        n_ref[...] = state[...].astype(BF16)


def line_adjoint_kernel(place_ref, *refs):
    y = place_ref[0]
    parts, rest = ring_parts(refs[:5]), refs[5:]
    ins, (out_ref, maps, held) = rest[:NY], rest[NY:]
    for k in range(NY):
        held[k] = ins[k][...]
        for h in range(H):
            maps[k, h] = parts[k][h][:, :DK]
    last = lax.rem(y + 1, NY)
    totals = [held[last, h].astype(F32) for h in range(H)]
    for j in range(NY - 2, -1, -1):
        k = lax.rem(y - j + NY, NY)
        for h in range(H):
            totals[h] = tn_two(maps[k, h], totals[h]) + held[k, h].astype(F32)
    for h in range(H):
        out_ref[h] = totals[h].astype(BF16)


def conv_backward(n, i, d_act, window, taps, carry, dx_ref, tail_ref, front_ref, taps_out_ref):
    conv = conv_apply(window, taps)
    s = jax.nn.sigmoid(conv)
    grad = d_act(conv * s) * (s * (1.0 + conv * (1.0 - s)))
    count, wide = grad.shape
    for j in range(TAPS):
        taps_out_ref[j : j + 1] += jnp.sum(
            grad * window[13 + j : 13 + j + count], 0, keepdims=True
        )
    longer = jnp.concatenate([grad, carry[...]], 0)
    d_x = longer[0:count] * taps[TAPS - 1 : TAPS]
    for j in range(TAPS - 1):
        d_x = d_x + longer[TAPS - 1 - j : TAPS - 1 - j + count] * taps[j : j + 1]
    dx_ref[:, :wide] = d_x.astype(BF16)
    carry[...] = grad[0:8]

    @pl.when(i == 0)
    def _():
        tail_ref[...] = d_x[count - 16 :]

    @pl.when(n == 0)
    def _():
        first = jnp.concatenate([jnp.zeros((16, wide), F32), grad[0:8]], 0)
        front = jnp.zeros((16, wide), F32)
        for j in range(TAPS - 1):
            front = front + first[TAPS - 1 - j : TAPS - 1 - j + 16] * taps[j : j + 1]
        front_ref[...] = front


def stacked(pieces, h):
    found = [piece for piece, (_, head) in zip(pieces, CHAINS) if head == h]
    return jnp.concatenate([piece.astype(BF16).astype(F32) for piece in found], 0)


def unit_back(raw, f):
    r = lax.rsqrt(jnp.sum(raw * raw, -1, keepdims=True) + EPSILON)
    unit = raw * r
    return (f - unit * jnp.sum(unit * f, -1, keepdims=True)) * r


def chunk_query_kernel(
    where_ref, x_ref, before_ref, edge_ref, taps_ref, q_ref, k_ref, gates_ref, p_ref, d_ref,
    s_ref, dm_ref,
    dx_ref, tail_ref, front_ref, taps_out_ref, dk_ref, dg_ref, carry,
):
    i = pl.program_id(0)
    n = pl.num_programs(0) - 1 - i
    row, col = iotas(C, C)
    chains = range(len(CHAINS))

    @pl.when(i == 0)
    def _():
        carry[...] = jnp.zeros_like(carry)
        taps_out_ref[...] = jnp.zeros_like(taps_out_ref)

    all_gates = [gates_ref[block(j)] for j in range(PAIR)]
    lines = [a.T for a in all_gates]
    g = [all_gates[j][:, h : h + 1] for j, h in CHAINS]
    growth = [jnp.exp(g[c]) for c in chains]
    qb = [q_ref[block(j), head_keys(h)] for j, h in CHAINS]
    kb = [k_ref[block(j), head_keys(h)] for j, h in CHAINS]
    dm = [dm_ref[block(j), head_values(h)] for j, h in CHAINS]
    d_p = [
        jnp.where(row >= col, nt(dm[c], d_ref[j, h]), 0.0) for c, (j, h) in enumerate(CHAINS)
    ]
    d_grown = [nt(dm[c], s_ref[j, h]) for c, (j, h) in enumerate(CHAINS)]
    ratio = [decay_ratio(g[c], lines[j][h : h + 1]) for c, (j, h) in enumerate(CHAINS)]
    d_score = [(d_p[c] * ratio[c]).astype(BF16) for c in chains]
    d_q = [mm(d_score[c], kb[c]) + growth[c] * d_grown[c] for c in chains]
    d_cumulative = [jnp.zeros((C, C), F32) for _ in range(PAIR)]
    for c, (j, h) in enumerate(CHAINS):
        dk_ref[j, h] = tn(d_score[c], qb[c])
        flow = d_p[c] * p_ref[j, h].astype(F32)
        d_g = jnp.sum(flow - flow.T, -1, keepdims=True) + jnp.sum(
            d_grown[c] * (qb[c].astype(F32) * growth[c]), -1, keepdims=True
        )
        d_cumulative[j] = jnp.where(col == h, d_g, d_cumulative[j])
    for j in range(PAIR):
        dg_ref[block(j)] = d_cumulative[j]
    window = conv_window(jnp.where(n == 0, edge_ref[...], before_ref[...]), x_ref[...])

    def d_act(act):
        return jnp.concatenate(
            [unit_back(act[:, head_keys(h)], stacked(d_q, h) * DK ** (-0.5)) for h in range(H)],
            1,
        )

    conv_backward(
        n, i, d_act, window, taps_ref[...], carry, dx_ref, tail_ref, front_ref, taps_out_ref
    )


def chunk_backward_kernel(where_ref, *refs):
    along, across, refs = ring_parts(refs[:5]), ring_parts(refs[5:10]), refs[10:]
    y_parts, z_parts, refs = refs[:3], refs[3:6], refs[6:]
    (xk_ref, xv_ref, bk_ref, bv_ref, ek_ref, ev_ref, ab_ref, taps_ref, rates_ref,
     k_ref, v_ref, gates_ref, t_ref, w_ref, u_ref, d_ref, s_ref, pd_ref, qd_ref, dkq_ref,
     dgq_ref,
     dx_ref, tail_ref, front_ref, taps_out_ref, rates_out_ref, state, carry) = refs
    i = pl.program_id(0)
    n = pl.num_programs(0) - 1 - i
    y, z = where_ref[1], where_ref[2]
    row, col = iotas(C, C)
    chains = range(len(CHAINS))

    @pl.when(i == 0)
    def _():
        s = [jnp.zeros((DK, DV), F32) for _ in range(H)]
        for place, maps, parts in ((z, across, z_parts), (y, along, y_parts)):
            for shift in (1, 2, 3):
                for h in range(H):
                    m = maps[shift][h][:, :DK]
                    new = tn_two(m, s[h]) + parts[shift - 1][h].astype(F32)
                    s[h] = jnp.where(place < shift, new, s[h])
        for h in range(H):
            state[h] = s[h]
        carry[...] = jnp.zeros_like(carry)
        taps_out_ref[...] = jnp.zeros_like(taps_out_ref)
        rates_out_ref[...] = jnp.zeros_like(rates_out_ref)

    all_gates = [gates_ref[block(j)] for j in range(PAIR)]
    lines = [a.T for a in all_gates]
    g = [all_gates[j][:, h : h + 1] for j, h in CHAINS]
    beta = [all_gates[j][:, H + h : H + h + 1] for j, h in CHAINS]
    total = [g[c][C - 1 : C] for c in chains]
    growth = [jnp.exp(g[c]) for c in chains]
    fade = [jnp.exp(total[c] - g[c]) for c in chains]
    kb = [k_ref[block(j), head_keys(h)] for j, h in CHAINS]
    k = [a.astype(F32) for a in kb]
    v = [v_ref[block(j), head_values(h)].astype(F32) for j, h in CHAINS]
    held = [s_ref[j, h] for j, h in CHAINS]
    delta = [d_ref[j, h] for j, h in CHAINS]
    w = [w_ref[j, h] for j, h in CHAINS]
    t = [t_ref[j, h] for j, h in CHAINS]
    trail = [k[c] * fade[c] for c in chains]
    old = [None] * len(CHAINS)
    d_delta = [None] * len(CHAINS)
    for c in reversed(chains):
        j, h = CHAINS[c]
        old[c] = state[h]
        d_delta[c] = (pd_ref[j, h] + mm(trail[c], old[c])).astype(BF16)
        state[h] = jnp.exp(total[c]) * old[c] + qd_ref[j, h] - tn(w[c], d_delta[c])
    old_b = [a.astype(BF16) for a in old]
    d_trail = [nt(delta[c], old_b[c]) for c in chains]
    d_w = [nt(d_delta[c], held[c]) for c in chains]
    d_wide_k = [-tn(t[c], d_w[c]) for c in chains]
    d_wide_v = [tn(t[c], d_delta[c]) for c in chains]
    ratio = [decay_ratio(g[c], lines[j][h : h + 1]) for c, (j, h) in enumerate(CHAINS)]
    gram = [nt(kb[c], kb[c]) for c in chains]
    a = [jnp.where(row > col, gram[c] * ratio[c], 0.0) for c in chains]
    d_system = [
        jnp.where(row > col, -(nt(d_wide_k[c], w[c]) + nt(d_wide_v[c], u_ref[j, h])), 0.0)
        for c, (j, h) in enumerate(CHAINS)
    ]
    d_a = [beta[c] * d_system[c] for c in chains]
    d_gram = [d_a[c] * ratio[c] for c in chains]
    both = [(d_gram[c] + d_gram[c].T).astype(BF16) for c in chains]
    d_k = [
        mm(both[c], kb[c])
        + dkq_ref[j, h]
        + (beta[c] * growth[c]) * d_wide_k[c]
        + fade[c] * d_trail[c]
        for c, (j, h) in enumerate(CHAINS)
    ]
    d_v = [beta[c] * d_wide_v[c] for c in chains]
    d_cumulative = [dgq_ref[block(j)] for j in range(PAIR)]
    d_beta = [jnp.zeros((C, C), F32) for _ in range(PAIR)]
    for c, (j, h) in enumerate(CHAINS):
        in_k = jnp.sum(d_wide_k[c] * k[c], -1, keepdims=True) * growth[c]
        in_v = jnp.sum(d_wide_v[c] * v[c], -1, keepdims=True)
        flow = d_a[c] * a[c]
        shed = jnp.sum(d_trail[c] * trail[c], -1, keepdims=True)
        last = jnp.sum(shed, 0, keepdims=True) + jnp.exp(total[c]) * jnp.sum(
            jnp.sum(old[c] * held[c].astype(F32), -1, keepdims=True), 0, keepdims=True
        )
        d_g = (
            jnp.sum(flow - flow.T, -1, keepdims=True)
            + beta[c] * in_k
            - shed
            + jnp.where(row[:, :1] == C - 1, last, 0.0)
        )
        d_b = jnp.sum(d_system[c] * a[c], -1, keepdims=True) + in_v + in_k
        d_cumulative[j] = jnp.where(col == h, d_cumulative[j] + d_g, d_cumulative[j])
        d_beta[j] = jnp.where(col == H + h, d_b, d_beta[j])
    rates = rates_ref[...]
    wide = taps_ref.shape[1]
    for j in range(PAIR):
        d_log = mm_ones((row <= col).astype(F32), d_cumulative[j])
        ab = ab_ref[block(j)]
        slope = rates[0:1] * jax.nn.sigmoid(ab + rates[1:2])
        log_decay = rates[0:1] * softplus(ab + rates[1:2])
        rates_out_ref[0:1] += jnp.sum(d_log * slope, 0, keepdims=True)
        rates_out_ref[1:2] += jnp.sum(d_log * log_decay, 0, keepdims=True)
        d_ab = d_log * slope + d_beta[j] * all_gates[j] * (1.0 - all_gates[j])
        dx_ref[block(j), wide : wide + 128] = d_ab.astype(BF16)
        dx_ref[block(j), wide + 128 :] = jnp.zeros((C, dx_ref.shape[1] - wide - 128), BF16)
    window = conv_window(
        jnp.concatenate(
            [
                jnp.where(n == 0, ek_ref[...], bk_ref[...]),
                jnp.where(n == 0, ev_ref[...], bv_ref[...]),
            ],
            1,
        ),
        jnp.concatenate([xk_ref[...], xv_ref[...]], 1),
    )

    def d_act(act):
        return jnp.concatenate(
            [unit_back(act[:, head_keys(h)], stacked(d_k, h)) for h in range(H)]
            + [stacked(d_v, h) for h in range(H)],
            1,
        )

    conv_backward(
        n, i, d_act, window, taps_ref[...], carry, dx_ref, tail_ref, front_ref, taps_out_ref
    )


def join_columns(x, parts, full_ref):
    own, one, top, bottom, three = parts
    half, width = top.shape

    def at(k):
        return pl.ds(pl.multiple_of(lax.rem(x - k + NX, NX) * width, 128), width)

    full_ref[:, at(0)] = own[...]
    full_ref[:, at(1)] = one[...]
    full_ref[:half, at(2)] = top[...]
    full_ref[half:, at(2)] = bottom[...]
    full_ref[:, at(3)] = three[...]


def gather_norm_kernel(place_ref, after_ref, gain_ref, *refs):
    parts, (full_ref, normed_ref) = refs[:5], refs[5:]
    join_columns(place_ref[0], parts, full_ref)
    for i in range(full_ref.shape[0] // 32):
        u = full_ref[i * 32 : (i + 1) * 32].astype(F32)
        r = lax.rsqrt(jnp.mean(u * u, -1, keepdims=True) + EPSILON)
        normed_ref[i * 32 : (i + 1) * 32] = (u * r * gain_ref[...]).astype(BF16)


def gather_kernel(place_ref, *refs):
    join_columns(place_ref[0], refs[:5], refs[5])


def norm_back_kernel(place_ref, after_ref, gain_ref, u_ref, dy_ref, *refs):
    parts, (d_ref, grad_ref, e_ref) = refs[:5], refs[5:]
    join_columns(place_ref[0], parts, e_ref)
    gain = gain_ref[...]
    total = jnp.zeros((8, u_ref.shape[1]), F32)
    for i in range(u_ref.shape[0] // 32):
        at = slice(i * 32, (i + 1) * 32)
        u = u_ref[at].astype(F32)
        e = e_ref[at].astype(F32)
        r = lax.rsqrt(jnp.mean(u * u, -1, keepdims=True) + EPSILON)
        n = u * r
        en = e * n
        d = r * (gain * e - n * jnp.mean(gain * en, -1, keepdims=True))
        d_ref[at] = (dy_ref[at].astype(F32) + d).astype(BF16)
        for j in range(4):
            total = total + en[j * 8 : (j + 1) * 8]
    grad_ref[...] = jnp.sum(total, 0, keepdims=True)


def pack_kernel(plan, place_ref, *refs):
    parts, (shard_ref, send_ref) = refs[:-2], refs[-2:]
    core = place_ref[0]
    first = core == 0
    height = send_ref.shape[0]
    mine = pl.ds(pl.multiple_of(core * height, height), height)
    at = 0
    for which, start, width, padded in plan:
        part = parts[which]
        half = part.shape[1] // NC
        low, high = part[:, start : start + width], part[:, half + start : half + start + width]
        for out, rows, value in (
            (shard_ref, mine, jnp.where(first, low, high)),
            (send_ref, slice(None), jnp.where(first, high, low)),
        ):
            out[rows, at : at + width] = value
            if padded > width:
                out[rows, at + width : at + padded] = jnp.zeros((height, padded - width), BF16)
        at += padded


def place_kernel(plan, ab_at, place_ref, total_ref, got_ref, *outs):
    core = place_ref[0]
    first = core == 0
    height = got_ref.shape[0]
    mine = pl.ds(pl.multiple_of(core * height, height), height)
    for out, cuts in zip(outs, plan):
        half = out.shape[1] // NC
        for start, to, width in cuts:
            own = total_ref[mine, start : start + width].astype(F32)
            got = got_ref[:, start : start + width].astype(F32)
            out[:, to : to + width] = jnp.where(first, own, got)
            out[:, half + to : half + to + width] = jnp.where(first, got, own)
    if ab_at is not None:
        own = total_ref[mine, ab_at : ab_at + 128].astype(F32)
        got = got_ref[:, ab_at : ab_at + 128].astype(F32)
        turned = jnp.concatenate([own, got], 0).T
        own, got = turned[: 2 * H, :height], turned[: 2 * H, height:]
        low, high = jnp.where(first, own, got), jnp.where(first, got, own)
        for out, start in zip(outs[len(plan) :], (0, H)):
            out[:H] = low[start : start + H]
            out[H:] = high[start : start + H]


def mlp_kernel(own_ref, other_ref, w_ref, d_inner_ref, inner_ref, d_gu_ref):
    x = jnp.concatenate([own_ref[...], other_ref[...]], 0)
    prod = mm(x, w_ref[...])
    width = inner_ref.shape[1]
    gate, up, d_inner = prod[:, :width], prod[:, width:], d_inner_ref[...]
    s = jax.nn.sigmoid(gate)
    act = gate * s
    inner_ref[...] = (act * up).astype(BF16)
    d_gu_ref[:, :width] = (d_inner * up * s * (1.0 + gate * (1.0 - s))).astype(BF16)
    d_gu_ref[:, width:] = (d_inner * act).astype(BF16)


def turn_kernel(*refs):
    at = 0
    for piece in refs[:-1]:
        rows = piece.shape[0]
        refs[-1][:, at : at + rows] = piece[...].T
        at += rows


def outer_kernel(plan, has_weights, *refs):
    refs = list(refs)
    j = pl.program_id(0)
    refs.pop(0)
    weight = refs.pop(0) if has_weights else None
    turned = [refs.pop() for pieces in [p for _, _, p, _, _ in plan][::-1] if pieces][::-1]
    acc = refs.pop() if has_weights else None
    out = refs.pop()
    if has_weights:

        @pl.when(j == 0)
        def _():
            acc[...] = jnp.zeros_like(acc)

    for first, count, pieces, has_front, has_weight in plan:
        if pieces:
            left = turned.pop(0)
            parts, refs = refs[:pieces], refs[pieces:]

            @pl.when(j == first)
            def _(left=left, parts=parts):
                turn_kernel(*parts, left)

        else:
            left = refs.pop(0)
        right = refs.pop(0)
        front = refs.pop(0) if has_front else None

        @pl.when((j >= first) & (j < first + count))
        def _(left=left, right=right, front=front, has_weight=has_weight):
            tokens, width = right.shape
            prod = mm(left[:, :tokens], right[...])
            if front is not None:
                prod = prod + mm(left[:, tokens:], front[...])
            out[...] = prod.astype(BF16)
            if has_weight:
                part = prod * weight[...].astype(F32)
                total = part[:, :128]
                for at in range(128, width, 128):
                    total = total + part[:, at : at + 128]
                acc[...] += total


def params(**more):
    return pltpu.CompilerParams(vmem_limit_bytes=VMEM, **more)


SMEM_SPEC = pl.BlockSpec(memory_space=pltpu.SMEM)
VMEM_SPEC = pl.BlockSpec(memory_space=pltpu.VMEM)
ANY_SPEC = pl.BlockSpec(memory_space=pl.ANY)


def whole_call(kernel, out_shape, place, *operands, scratch=(), after=None, flops=0):
    many = isinstance(out_shape, (tuple, list))
    first = [] if place is None else [place]
    first_specs = [] if place is None else [SMEM_SPEC]
    if after is not None:
        first, first_specs = first + [after], first_specs + [ANY_SPEC]
    outs = out_shape if many else [out_shape]
    moved = sum(v.size * v.dtype.itemsize for v in operands)
    moved += sum(o.size * o.dtype.itemsize for o in outs)
    return pl.pallas_call(
        kernel,
        out_shape=out_shape,
        in_specs=first_specs + [VMEM_SPEC] * len(operands),
        out_specs=[VMEM_SPEC] * len(out_shape) if many else VMEM_SPEC,
        scratch_shapes=list(scratch),
        compiler_params=params(),
        cost_estimate=pl.CostEstimate(
            flops=flops or moved, bytes_accessed=moved, transcendentals=0
        ),
    )(*first, *operands)


def sds(shape, dtype):
    return jax.ShapeDtypeStruct(shape, dtype)


def outer_call(pairs, tile, start, into, after=None, weight=None):
    tokens = pairs[0][1].shape[0]
    scratch = []
    fresh = isinstance(into, int)
    some = pairs[0][0]
    height = some[0].shape[1] if isinstance(some, tuple) else some.shape[0]
    shape = (height, into) if fresh else into.shape
    specs, operands, plan = [ANY_SPEC], [after if fresh else into], []
    counts = [right.shape[1] // tile for _, right, _, _ in pairs]
    firsts = [sum(counts[:i]) for i in range(len(pairs))]
    if weight is not None:

        def weight_index(j):
            column = 0
            for (_, _, _, at), first, count in zip(pairs, firsts, counts):
                if at is not None:
                    inside = jnp.clip(j - first, 0, count - 1)
                    column = jnp.where(j >= first, at + inside * tile, column)
            return 0, pl.multiple_of(column, 128)

        specs.append(pl.BlockSpec((pl.Element(height), pl.Element(tile)), weight_index))
        operands.append(weight)
    for (left, right, front, at), first, count in zip(pairs, firsts, counts):

        def index(j, first=first, count=count):
            return 0, jnp.clip(j - first, 0, count - 1)

        pieces = left if isinstance(left, tuple) else (left,)
        for piece in pieces:
            specs.append(pl.BlockSpec(piece.shape, lambda j: (0, 0)))
        specs.append(pl.BlockSpec((tokens, tile), index))
        operands += [*pieces, right]
        if isinstance(left, tuple):
            scratch.append(pltpu.VMEM((height, tokens), BF16))
        if front is not None:
            specs.append(pl.BlockSpec((front.shape[0], tile), index))
            operands.append(front)
        turning = len(pieces) if isinstance(left, tuple) else 0
        plan.append((first, count, turning, front is not None, at is not None))
    out_shape = [sds(shape, BF16)]
    out_specs = [
        pl.BlockSpec((pl.Element(height), pl.Element(tile)), lambda j: (0, pl.multiple_of(start + j * tile, 128)))
    ]
    if weight is not None:
        out_shape.append(sds((height, 128), F32))
        out_specs.append(pl.BlockSpec((height, 128), lambda j: (0, 0)))
    width = sum(counts) * tile
    out = pl.pallas_call(
        partial(outer_kernel, plan, weight is not None),
        out_shape=out_shape,
        grid=(sum(counts),),
        in_specs=specs,
        out_specs=out_specs,
        scratch_shapes=scratch,
        input_output_aliases={} if fresh else {0: 0},
        compiler_params=params(dimension_semantics=("arbitrary",)),
        cost_estimate=pl.CostEstimate(
            flops=2 * tokens * height * width,
            bytes_accessed=2 * height * width + 4 * tokens * height,
            transcendentals=0,
        ),
    )(*operands)
    return out if weight is not None else out[0]


def on_chips(v, target):
    pairs = []
    for z in range(NZ):
        for y in range(NY):
            for c in range(NC):
                to_z, to_y, to_c = target(z, y, c)
                pairs.append(((z * NY + y) * NC + c, (to_z * NY + to_y) * NC + to_c))
    return lax.ppermute(v, "seq", pairs)


def core_swap(v):
    return on_chips(v, lambda z, y, c: (z, y, 1 - c))


def along_y(v, shift):
    return on_chips(v, lambda z, y, c: (z, (y + shift) % NY, c))


def along_z(v, shift):
    return on_chips(v, lambda z, y, c: ((z + shift) % NZ, y, c))


def along_x(v, shift):
    return lax.ppermute(v, "head", [(i, (i + shift) % NX) for i in range(NX)])


def next_chip(v, step):
    count = NZ * NY * NC
    return lax.ppermute(
        v, "seq", [(i, i + NC * step) for i in range(count) if 0 <= i + NC * step < count]
    )


GROUPS = [[c + NC * j for j in range(NZ * NY)] for c in range(NC)]


def gather_chips(shard):
    return lax.all_gather(shard, "seq", axis=0, tiled=True, axis_index_groups=GROUPS)


def scatter_chips(full):
    return lax.psum_scatter(
        full, "seq", scatter_dimension=0, tiled=True, axis_index_groups=GROUPS
    )


def ring_gather(move, v):
    half = v.shape[0] // 2
    one, three = move(v, 1), move(v, -1)
    return v, one, move(one[:half], 1), move(three[half:], -1), three


def ring_direct(move, v):
    return [v] + [move(v, k) for k in (1, 2, 3)]


def reduce_features(rows_in, dot, x):
    half = rows_in.shape[0] // 2
    arrived = core_swap(dot(rows_in[half:]).astype(BF16))
    own = dot(rows_in[:half]).astype(BF16)
    width = own.shape[1] // NX

    def cut(distance):
        at = (0, lax.rem(x + distance, NX) * width)
        mine = lax.dynamic_slice(own, at, (half, width))
        return mine.astype(F32) + lax.dynamic_slice(arrived, at, (half, width)).astype(F32)

    got = [along_x(cut(k).astype(BF16), k) for k in (2, 1, 3)]
    total = cut(0)
    for part in got:
        total = total + part.astype(F32)
    return total


def plain_dot(left_op, right_op):
    return jnp.dot(left_op, right_op, preferred_element_type=F32)


def dot_last(left_op, right_op):
    return lax.dot_general(
        left_op, right_op, (((1,), (1,)), ((), ())), preferred_element_type=F32
    )


def on_device(
    hidden_in, out_grad, norm_attn, w_query, w_key, w_value, conv_query, conv_key, conv_value,
    w_alpha, w_beta, log_rate, rate_bias, w_gate_out, head_norm, w_out, norm_mlp,
    w_mlp_gate, w_mlp_up, w_mlp_down,
):
    seq = lax.axis_index("seq")
    x = lax.axis_index("head")
    core = seq % NC
    chip = seq // NC
    y, z = chip % NY, chip // NY
    first_core = core == 0
    rows, slice_width = hidden_in.shape
    wide = slice_width * NX
    tokens = rows * NC
    steps = tokens // ROWS
    blocks = tokens // C
    keys = H * DK
    vals = H * DV
    ff = w_mlp_gate.shape[1] // NC
    ff_pad = -(-ff // 128) * 128
    qkv = 2 * keys + vals
    qkv_ab = qkv + 128
    place_x = jnp.stack([x]).astype(jnp.int32)
    place_y = jnp.stack([y]).astype(jnp.int32)
    place = jnp.stack([core, y, z]).astype(jnp.int32)
    place_core = jnp.stack([core]).astype(jnp.int32)

    def gathered(parts, plan):
        height, width = parts[0].shape[0], sum(padded for _, _, _, padded in plan)
        shard, send = whole_call(
            partial(pack_kernel, plan),
            [sds((NC * height, width), BF16), sds((height, width), BF16)], place_core, *parts,
        )
        shard = lax.dynamic_update_slice(shard, core_swap(send), ((1 - core) * height, 0))
        return shard, gather_chips(shard)

    ab = jnp.concatenate(
        [w.T[c * H : (c + 1) * H] for c in range(NC) for w in (w_alpha, w_beta)], 0
    ).T
    shard, full = gathered(
        [w_query, w_key, w_value, ab, w_gate_out, w_out.T],
        [
            (0, 0, keys, keys), (1, 0, keys, keys), (2, 0, vals, vals), (3, 0, 2 * H, 128),
            (4, 0, vals, vals), (5, 0, vals, vals),
        ],
    )
    w_gate, w_attn = full[:, qkv_ab : qkv_ab + vals], full[:, qkv_ab + vals :]
    cuts = [(i * 256, min(256, ff - i * 256)) for i in range(ff_pad // 256)]
    later, _ = lax.optimization_barrier(((w_mlp_gate, w_mlp_up, w_mlp_down.T), shard))
    _, full_mlp = gathered(
        later,
        [(which, start, width, 256) for start, width in cuts for which in (0, 1)]
        + [(2, start, width, 256) for start, width in cuts],
    )
    w_gu, w_dn = full_mlp[:, : 2 * ff_pad], full_mlp[:, 2 * ff_pad :]

    gain_one = norm_attn.reshape(1, wide)
    gain_two = norm_mlp.reshape(1, wide)
    full_in, normed_own = whole_call(
        gather_norm_kernel, [sds((rows, wide), BF16)] * 2, place_x, gain_one,
        *ring_gather(along_x, hidden_in), after=gain_one,
    )
    normed_other = core_swap(normed_own)
    halo = next_chip(
        jnp.where(first_core, normed_other[rows - 16 :], normed_own[rows - 16 :]), 1
    )
    normed = jnp.concatenate([normed_own, normed_other, halo], 0)
    dy_own = whole_call(
        gather_kernel, sds((rows, wide), BF16), place_x,
        *ring_gather(along_x, out_grad),
    )
    dy_other = core_swap(dy_own)
    full_dy = jnp.concatenate([dy_own, dy_other], 0)
    normed_t = whole_call(
        turn_kernel, sds((wide, tokens + 16), BF16), None, normed_own, normed_other, halo
    )
    dy_t = whole_call(turn_kernel, sds((wide, tokens), BF16), None, dy_own, dy_other)
    normed, full_dy, normed_t, dy_t = lax.optimization_barrier((normed, full_dy, normed_t, dy_t))

    proj = plain_dot(normed, full[:, :qkv_ab])
    gate_in = plain_dot(normed, w_gate)

    def conv_half(w):
        width = w.shape[1] // NC
        return lax.dynamic_slice_in_dim(w, core * width, width, 1)

    taps_all = jnp.pad(
        jnp.concatenate(
            [conv_half(conv_query), conv_half(conv_key), conv_half(conv_value)], 1
        ).astype(F32),
        ((0, 8 - TAPS), (0, 0)),
    )
    rate_rows = jnp.stack([-jnp.exp(log_rate), rate_bias])
    rates = jnp.pad(
        lax.dynamic_slice_in_dim(rate_rows, core * H, H, 1), ((0, 6), (0, 128 - H))
    )
    head_gain = head_norm.reshape(1, DV)

    def at(n, where):
        return lax.rem(n + steps // NC * where[0], steps)

    def rows_spec(width, backward=False, col=0):
        if backward:
            return pl.BlockSpec((ROWS, width), lambda i, s: (at(steps - 1 - i, s), col))
        return pl.BlockSpec((ROWS, width), lambda i, s: (at(i, s), col))

    def before_spec(width, backward=False, col=0):
        def index(i, s):
            n = steps - 1 - i if backward else i
            return (at(jnp.maximum(n - 1, 0), s) * (ROWS // 16) + ROWS // 16 - 1, col)

        return pl.BlockSpec((16, width), index)

    def chain_spec(cols, backward=False):
        if backward:
            return pl.BlockSpec((PAIR, H, C, cols), lambda i, s: (steps - 1 - i, 0, 0, 0))
        return pl.BlockSpec((PAIR, H, C, cols), lambda i, s: (i, 0, 0, 0))

    def full_spec(*shape):
        zeros = (0,) * len(shape)
        return pl.BlockSpec(shape, lambda i, s: zeros)

    edge_spec = pl.BlockSpec((16, qkv), lambda i, s: (tokens // 16, 0))

    def chunk_call(kernel, in_specs, outs, scratch, *operands):
        return pl.pallas_call(
            kernel,
            out_shape=[o for o, _ in outs],
            grid_spec=pltpu.PrefetchScalarGridSpec(
                num_scalar_prefetch=1,
                grid=(steps,),
                in_specs=in_specs,
                out_specs=[spec for _, spec in outs],
                scratch_shapes=scratch,
            ),
            compiler_params=params(dimension_semantics=("arbitrary",)),
        )(place, *operands)

    map_shape, part_shape = (DK, DK + DV), (DK, DV)
    q_n, k_n, v_n, gates, p_c, t_c, w_c, u_c, own_map = chunk_call(
        chunk_forward_kernel,
        [
            rows_spec(qkv), before_spec(qkv), edge_spec, rows_spec(128, col=qkv // 128),
            full_spec(8, qkv), full_spec(8, 128),
        ],
        [
            (sds((tokens, keys), BF16), rows_spec(keys)),
            (sds((tokens, keys), BF16), rows_spec(keys)),
            (sds((tokens, vals), BF16), rows_spec(vals)),
            (sds((tokens, 128), F32), rows_spec(128)),
            (sds((blocks, H, C, C), BF16), chain_spec(C)),
            (sds((blocks, H, C, C), BF16), chain_spec(C)),
            (sds((blocks, H, C, DK), BF16), chain_spec(DK)),
            (sds((blocks, H, C, DV), F32), chain_spec(DV)),
            (sds((H,) + map_shape, BF16), full_spec(H, *map_shape)),
        ],
        [pltpu.VMEM((H,) + map_shape, F32)],
        proj, proj, proj, proj, taps_all, rates,
    )
    y_maps = ring_gather(along_y, own_map)
    line_map = whole_call(
        line_map_kernel, sds((H,) + map_shape, BF16), place_y, *y_maps,
        scratch=[pltpu.VMEM((NY, H) + map_shape, BF16)],
    )
    z_maps = ring_gather(along_z, line_map)
    map_specs = [full_spec(h, *map_shape) for h in (H, H, 1, 1, H)] * 2
    mixed, attn, d_c, s_c = chunk_call(
        chunk_output_kernel,
        map_specs
        + [
            rows_spec(keys), rows_spec(keys), rows_spec(128), chain_spec(C), chain_spec(DK),
            chain_spec(DV), rows_spec(vals), full_spec(1, DV),
        ],
        [
            (sds((tokens, vals), F32), rows_spec(vals)),
            (sds((tokens, vals), BF16), rows_spec(vals)),
            (sds((blocks, H, C, DV), BF16), chain_spec(DV)),
            (sds((blocks, H, DK, DV), BF16), chain_spec(DV)),
        ],
        [pltpu.VMEM((H,) + part_shape, F32)],
        *y_maps, *z_maps, q_n, k_n, gates, p_c, w_c, u_c, gate_in, head_gain,
    )
    attn_part = reduce_features(attn, lambda v: dot_last(v, w_attn), x)
    middle = (hidden_in.astype(F32) + attn_part).astype(BF16)

    d_inner = plain_dot(full_dy, w_dn)
    full_middle, normed_two_own = whole_call(
        gather_norm_kernel, [sds((rows, wide), BF16)] * 2, place_x, gain_two,
        *ring_gather(along_x, middle), after=d_inner,
    )
    normed_two_other = core_swap(normed_two_own)
    inner, d_gu = pl.pallas_call(
        mlp_kernel,
        out_shape=[sds((tokens, ff_pad), BF16), sds((tokens, 2 * ff_pad), BF16)],
        grid=(ff_pad // 256,),
        in_specs=[
            pl.BlockSpec((rows, wide), lambda j: (0, 0)),
            pl.BlockSpec((rows, wide), lambda j: (0, 0)),
            pl.BlockSpec((wide, 512), lambda j: (0, j)),
            pl.BlockSpec((tokens, 256), lambda j: (0, j)),
        ],
        out_specs=[
            pl.BlockSpec((tokens, 256), lambda j: (0, j)),
            pl.BlockSpec((tokens, 512), lambda j: (0, j)),
        ],
        compiler_params=params(dimension_semantics=("arbitrary",)),
    )(normed_two_own, normed_two_other, full_mlp, d_inner)
    d_two = reduce_features(d_gu, lambda v: dot_last(v, w_gu), x)
    mlp_grads = outer_call(
        [((normed_two_own, normed_two_other), d_gu, None, None), (dy_t, inner, None, None)],
        256, 0, 3 * ff_pad,
        after=d_gu,
    )
    mlp_grads, d_two = lax.optimization_barrier((mlp_grads, d_two))
    mlp_summed = scatter_chips(mlp_grads)
    d_middle_own, grad_norm_mlp = whole_call(
        norm_back_kernel, [sds((rows, wide), BF16), sds((1, wide), F32)], place_x,
        gain_two, full_middle, dy_own, *ring_gather(along_x, d_two.astype(BF16)),
        scratch=[pltpu.VMEM((rows, wide), BF16)], after=mlp_grads,
    )
    d_middle_other = core_swap(d_middle_own)

    wa_spec = pl.BlockSpec(
        (pl.Element(wide), pl.Element(vals)), lambda i, s: (0, qkv_ab + vals)
    )
    dm, d_gate_in, grad_head_norm, p_dm, q_dm, own_part = chunk_call(
        chunk_adjoint_kernel,
        [
            full_spec(rows, wide), full_spec(rows, wide), wa_spec,
            rows_spec(vals, True), rows_spec(vals, True), full_spec(1, DV),
            rows_spec(keys, True), rows_spec(keys, True), rows_spec(128, True),
            chain_spec(C, True), chain_spec(DK, True),
        ],
        [
            (sds((tokens, vals), BF16), rows_spec(vals, True)),
            (sds((tokens, vals), BF16), rows_spec(vals, True)),
            (sds((8, DV), F32), full_spec(8, DV)),
            (sds((blocks, H, C, DV), F32), chain_spec(DV, True)),
            (sds((blocks, H, DK, DV), F32), chain_spec(DV, True)),
            (sds((H,) + part_shape, BF16), full_spec(H, *part_shape)),
        ],
        [pltpu.VMEM((H,) + part_shape, F32)],
        d_middle_own, d_middle_other, full, mixed, gate_in, head_gain, q_n, k_n, gates, p_c, w_c,
    )
    y_parts = ring_direct(along_y, own_part)
    taps_q, taps_kv = taps_all[:, :keys], taps_all[:, keys:]
    kv = keys + vals

    def window_specs(width, col):
        return [
            rows_spec(width, True, col), before_spec(width, True, col),
            pl.BlockSpec((16, width), lambda i, s: (tokens // 16, col)),
        ]

    d_xq, tail_q, front_q, grad_taps_q, d_kq, d_gq = chunk_call(
        chunk_query_kernel,
        window_specs(keys, 0)
        + [
            full_spec(8, keys), rows_spec(keys, True), rows_spec(keys, True),
            rows_spec(128, True), chain_spec(C, True), chain_spec(DV, True),
            chain_spec(DV, True), rows_spec(vals, True),
        ],
        [
            (sds((tokens, keys), BF16), rows_spec(keys, True)),
            (sds((16, keys), F32), full_spec(16, keys)),
            (sds((16, keys), F32), full_spec(16, keys)),
            (sds((8, keys), F32), full_spec(8, keys)),
            (sds((blocks, H, C, DK), F32), chain_spec(DK, True)),
            (sds((tokens, 128), F32), rows_spec(128, True)),
        ],
        [pltpu.VMEM((8, keys), F32)],
        proj, proj, proj, taps_q, q_n, k_n, gates, p_c, d_c, s_c, dm,
    )
    line_part = whole_call(
        line_adjoint_kernel, sds((H,) + part_shape, BF16), place_y, *y_maps, *y_parts,
        scratch=[
            pltpu.VMEM((NY, H, DK, DK), BF16), pltpu.VMEM((NY, H) + part_shape, BF16),
        ],
    )
    z_parts = ring_direct(along_z, line_part)
    rest = kv + 256
    some_grads, gain_a = outer_call(
        [
            (normed_t, d_xq, front_q, 0), (normed_t, d_gate_in, None, qkv_ab),
            ((d_middle_own, d_middle_other), attn, None, None),
        ],
        256, rest, rest + keys + 2 * vals, after=own_part, weight=full,
    )
    part_specs = [full_spec(H, *part_shape)] * 6
    x_specs = [spec for pair in zip(window_specs(keys, 1), window_specs(vals, 1)) for spec in pair]
    d_xkv, tail, front, grad_taps_kv, grad_rates = chunk_call(
        chunk_backward_kernel,
        map_specs
        + part_specs
        + x_specs
        + [
            rows_spec(128, True, qkv // 128), full_spec(8, kv), full_spec(8, 128),
            rows_spec(keys, True), rows_spec(vals, True), rows_spec(128, True),
            chain_spec(C, True), chain_spec(DK, True), chain_spec(DV, True),
            chain_spec(DV, True), chain_spec(DV, True), chain_spec(DV, True),
            chain_spec(DV, True), chain_spec(DK, True), rows_spec(128, True),
        ],
        [
            (sds((tokens, rest), BF16), rows_spec(rest, True)),
            (sds((16, kv), F32), full_spec(16, kv)),
            (sds((16, kv), F32), full_spec(16, kv)),
            (sds((8, kv), F32), full_spec(8, kv)),
            (sds((8, 128), F32), full_spec(8, 128)),
        ],
        [pltpu.VMEM((H,) + part_shape, F32), pltpu.VMEM((8, kv), F32)],
        *y_maps, *z_maps, *y_parts[1:], *z_parts[1:],
        proj, proj, proj, proj, proj, proj, proj, taps_kv, rates, k_n, v_n, gates, t_c, w_c, u_c,
        d_c, s_c, p_dm, q_dm, d_kq, d_gq,
    )

    last_grads, gain_b = outer_call(
        [(normed_t, d_xkv, jnp.pad(front, ((0, 0), (0, rest - kv))), keys)], 256, 0, some_grads,
        weight=full,
    )
    summed = scatter_chips(last_grads)
    norm_attn_part = jnp.sum(gain_a + gain_b, 1) / norm_attn

    fixed = jnp.concatenate([tail_q, tail], 1) + next_chip(
        jnp.concatenate([front_q, front], 1), -1
    )
    last_at = jnp.where(first_core, tokens - 16, rows - 16)
    d_all = lax.dynamic_update_slice(
        jnp.concatenate([d_xq, d_xkv[:, : kv + 128], d_gate_in], 1), fixed.astype(BF16), (last_at, 0)
    )
    d_one = reduce_features(
        d_all, lambda v: dot_last(v, full[:, : qkv_ab + vals]), x
    )
    u = full_in.astype(F32)
    factor = lax.rsqrt(jnp.mean(u * u, -1, keepdims=True) + EPSILON)
    own_gain = lax.dynamic_slice_in_dim(gain_one, x * slice_width, slice_width, 1)
    n_own = hidden_in.astype(F32) * factor
    row_sum = jnp.sum(d_one * n_own * own_gain, -1).reshape(2, rows // 2)
    row_sum = row_sum + (along_x(row_sum, 1) + along_x(row_sum, 2) + along_x(row_sum, 3))
    row_mean = row_sum.reshape(rows, 1) / wide
    d_middle_cols = lax.dynamic_slice_in_dim(d_middle_own, x * slice_width, slice_width, 1)
    grad_input = (
        d_middle_cols.astype(F32) + factor * (d_one * own_gain - n_own * row_mean)
    ).astype(BF16)
    inner_late, _ = lax.optimization_barrier((inner, d_one))
    mlp_part = reduce_features(inner_late, lambda v: dot_last(v, w_dn), x)
    output = (middle.astype(F32) + mlp_part).astype(BF16)

    def placed(v, index, count):
        return jnp.where(jnp.arange(count).reshape((count,) + (1,) * v.ndim) == index, v[None], 0.0)

    shared = jnp.concatenate([norm_attn_part, grad_head_norm[0]]).reshape(-1, 128)
    shared = shared + (along_x(shared, 1) + along_x(shared, 2) + along_x(shared, 3))
    per_core = placed(
        jnp.concatenate(
            [
                jnp.concatenate([grad_taps_q, grad_taps_kv], 1)[:TAPS].reshape(-1),
                grad_rates[:2].reshape(-1),
            ]
        ),
        core, NC,
    ).reshape(-1, 128)
    split_a = shared.shape[0]
    split_b = split_a + per_core.shape[0]
    small = jnp.concatenate([shared, per_core, grad_norm_mlp.reshape(-1, 128)], 0)
    small = small + core_swap(small)
    small = small + (along_y(small, 1) + along_y(small, 2) + along_y(small, 3))
    small = small + (along_z(small, 1) + along_z(small, 2) + along_z(small, 3))
    grad_norm_attn = small[:split_a].reshape(-1)[:wide]
    grad_head_norm = small[:split_a].reshape(-1)[wide : wide + DV]
    cores = small[split_a:split_b].reshape(NC, -1)
    conv = cores[:, : TAPS * qkv].reshape(NC, TAPS, qkv)
    rate_sums = cores[:, TAPS * qkv :].reshape(NC, 2, 128)[:, :, :H]

    def joined(part):
        return jnp.swapaxes(part, 0, 1).reshape(TAPS, -1)

    grad_conv_query = joined(conv[:, :, :keys])
    grad_conv_key = joined(conv[:, :, keys : 2 * keys])
    grad_conv_value = joined(conv[:, :, 2 * keys :])
    grad_rate_bias = rate_sums[:, 0].reshape(-1)
    grad_log_rate = rate_sums[:, 1].reshape(-1)
    grad_norm_mlp = small[split_b:].reshape(-1)

    def placed_rows(total, plan, ab_at=None):
        height = total.shape[0] // NC
        got = core_swap(lax.dynamic_slice_in_dim(total, (1 - core) * height, height, 0))
        shapes = [sds((height, NC * width), F32) for width, _ in plan]
        if ab_at is not None:
            shapes += [sds((NC * H, height), F32)] * 2
        return whole_call(
            partial(place_kernel, [cuts for _, cuts in plan], ab_at), shapes, place_core, total,
            got,
        )

    grad_mlp_gate, grad_mlp_up, grad_down_t = placed_rows(
        mlp_summed,
        [
            (ff, [(2 * start, start, width) for start, width in cuts]),
            (ff, [(2 * start + 256, start, width) for start, width in cuts]),
            (ff, [(2 * ff_pad, 0, ff)]),
        ],
    )
    done = (
        output, grad_input, grad_norm_attn, grad_conv_query, grad_conv_key, grad_conv_value,
        grad_log_rate, grad_rate_bias, grad_head_norm, grad_norm_mlp, grad_mlp_gate, grad_mlp_up,
        grad_down_t,
    )
    summed, done = lax.optimization_barrier((summed, done))
    (
        output, grad_input, grad_norm_attn, grad_conv_query, grad_conv_key, grad_conv_value,
        grad_log_rate, grad_rate_bias, grad_head_norm, grad_norm_mlp, grad_mlp_gate, grad_mlp_up,
        grad_down_t,
    ) = done
    grad_key, grad_value, grad_query, grad_gate_out, grad_out_t, grad_alpha_t, grad_beta_t = (
        placed_rows(
            summed,
            [
                (keys, [(0, 0, keys)]), (vals, [(keys, 0, vals)]), (keys, [(rest, 0, keys)]),
                (vals, [(rest + keys, 0, vals)]), (vals, [(rest + keys + vals, 0, vals)]),
            ],
            kv,
        )
    )
    grad_alpha, grad_beta = grad_alpha_t.T, grad_beta_t.T
    grad_mlp_down, grad_out = grad_down_t.T, grad_out_t.T
    return (
        output, grad_input, grad_norm_attn, grad_query, grad_key, grad_value,
        grad_conv_query, grad_conv_key, grad_conv_value, grad_alpha, grad_beta,
        grad_log_rate, grad_rate_bias, grad_gate_out, grad_head_norm, grad_out,
        grad_norm_mlp, grad_mlp_gate, grad_mlp_up, grad_mlp_down,
    )


def solution(mesh):
    rows, columns = P("seq", "head"), P("head", "seq")
    taps, heads, whole = P(None, "head"), P("head"), P()
    return jax.shard_map(
        on_device,
        mesh=mesh,
        in_specs=(
            rows, rows, whole, rows, rows, rows, taps, taps, taps, rows, rows, heads, heads,
            rows, whole, columns, whole, rows, rows, columns,
        ),
        out_specs=(
            rows, rows, whole, rows, rows, rows, taps, taps, taps, rows, rows, heads, heads,
            rows, whole, columns, whole, rows, rows, columns,
        ),
        check_vma=False,
    )
```
